256 devices in a mesh: clip: 4 (over y_lo, core), seq: 64 (over z, y_hi, x).
Axes of the slice: x: 4, y: 4 (y_hi: 2, y_lo: 2; y = y_hi * 2 + y_lo), z: 8, core: 2. Of those that a mesh axis runs over, the one named last changes fastest.
Arguments:
- queries: bfloat16 [4, 32768, 3072], P('clip', 'seq'), may hold values from -6 to 6
- grad_out: bfloat16 [4, 32768, 3072], P('clip', 'seq'), may hold values from -6 to 6
- kept_pos: int32 [4, 32768], P('clip', 'seq'), may hold values from 0 to 511, as said below
- kept_count: int32 [4, 64], P('clip'), may hold values from 1 to 512, as said below
- caption_len: int32 [4], P('clip'), may hold values from 256 to 512, as said below
- cap_keys: bfloat16 [4, 512, 3072], P('clip', 'seq'), may hold values from -150 to 150
- cap_values: bfloat16 [4, 512, 3072], P('clip', 'seq'), may hold values from -6 to 6
- query_gain: float32 [3072], replicated, may hold values from 0.5 to 1.5
Outputs:
- query_grad: bfloat16 [4, 32768, 3072], P('clip', 'seq')
- key_grad: bfloat16 [4, 512, 3072], P('clip', 'seq')
- value_grad: bfloat16 [4, 512, 3072], P('clip', 'seq')
- gain_grad: float32 [3072], P('clip')
The draws below stay inside these ranges and needn't reach their ends.
Inputs may be any that keep to these rules, and one draw needn't show every extreme that they name: `kept_pos`: for each clip and each device along seq, its 512 entries are a permutation of 0 to 511: first the positions of its kept rows in ascending order, then the other positions in ascending order. `kept_count`: in every clip some device keeps all 512 tokens. `caption_len`: some clip has all 512 caption tokens.
All inputs are finite; a program needn't handle non-finite values.
Results may differ from the reference program's by a relative error of at most 0.005.
The reference program's roundings to bfloat16 on the way (of `live_grad`, `q_normed`, `probs_bf`, `dscores` and `dinput`) count: a program that leaves them out, or rounds other values in their place, can miss the bound.
Values may be sent and summed in bfloat16 or wider, within the bound.
No kernel may reach another device: no remote copies, remote signals or barrier semaphores. Data moves between devices by JAX's collectives and lax.ppermute only.
A program may use at most 192 MiB of HBM per device.

```python
import math
import jax
import jax.numpy as jnp
from jax import lax

HEADS = 24
HEAD_DIM = 128
SHARD = 512
FEAT = 3072
CLIPS = 4
TOKENS = 32768
CAP = 512
N_SEQ = 64


def caption_base(key):
    return jax.random.normal(jax.random.fold_in(key, 11), (CLIPS, CAP, HEADS * HEAD_DIM), jnp.float32)


def kept_layout(key):
    shard_total = TOKENS // SHARD
    first, second, third = jax.random.split(jax.random.fold_in(key, 21), 3)
    raw = jax.random.randint(first, (CLIPS, shard_total), 0, SHARD + 1)
    counts = jnp.maximum(1, raw * raw // SHARD)
    full_at = jax.random.randint(second, (CLIPS, 1), 0, shard_total)
    counts = jnp.where(jnp.arange(shard_total)[None, :] == full_at, SHARD, counts)
    scores = jax.random.randint(third, (CLIPS, shard_total, SHARD), 0, 2 ** 19) * SHARD + jnp.arange(SHARD)
    order = jnp.argsort(scores, axis=-1)
    ranking = jnp.argsort(order, axis=-1)
    dropped = (ranking >= counts[:, :, None]).astype(jnp.int32)
    sort_key = dropped * SHARD + jnp.arange(SHARD)
    positions = jnp.sort(sort_key, axis=-1) % SHARD
    return (counts.astype(jnp.int32), positions.reshape(CLIPS, TOKENS).astype(jnp.int32))


def draw_kept_pos(key, part):
    counts, positions = kept_layout(key)
    return positions


def draw_kept_count(key, part):
    counts, positions = kept_layout(key)
    return counts


def draw_caption_len(key, part):
    key = jax.random.fold_in(key, 5)
    first, second = jax.random.split(key)
    lengths = jax.random.randint(first, (CLIPS,), CAP // 2, CAP + 1)
    full_at = jax.random.randint(second, (1,), 0, CLIPS)
    return jnp.where(jnp.arange(CLIPS) == full_at, CAP, lengths).astype(jnp.int32)


def draw_cap_keys(key, part):
    base = caption_base(key)
    return jnp.clip(base * 3.0, -150.0, 150.0).astype(jnp.bfloat16)


def draw_queries(key, part):
    key = jax.random.fold_in(key, 2)
    vals = jax.random.normal(key, (CLIPS, TOKENS, HEADS * HEAD_DIM), jnp.float32)
    return jnp.clip(vals, -6.0, 6.0).astype(jnp.bfloat16)


def steps_of(own_key, dims, cuts, smallest, largest):
    level, own = 1.0, jax.random.fold_in(own_key, 6)
    for position, parts in cuts:
        steps = jnp.exp(jax.random.uniform(jax.random.fold_in(own, position), (parts,), jnp.float32, smallest / len(cuts), largest / len(cuts)))
        level = level * jnp.repeat(steps, dims[position] // parts).reshape([-1 if axis == position else 1 for axis in range(len(dims))])
    return level


def gaussian(own_key, dims, deviation, limit, shards=(), dtype=jnp.bfloat16):
    gain = steps_of(own_key, dims, shards, -0.22, 0.18) if shards else 1.0
    values = jax.random.normal(own_key, dims, jnp.float32) * deviation * gain
    return jnp.minimum(jnp.maximum(values, -limit), limit).astype(dtype)


def setup_inputs(seed: int = 0) -> dict:
    keys = jax.random.split(jax.random.key(seed), 9)
    return {
        "queries": draw_queries(jax.random.fold_in(keys[8], 71), 0),
        "grad_out": gaussian(keys[1], (CLIPS, TOKENS, FEAT), 1.0, 6.0, ((0, 4), (1, 64))),
        "kept_pos": draw_kept_pos(jax.random.fold_in(keys[8], 71), 0),
        "kept_count": draw_kept_count(jax.random.fold_in(keys[8], 71), 0),
        "caption_len": draw_caption_len(jax.random.fold_in(keys[8], 71), 0),
        "cap_keys": draw_cap_keys(jax.random.fold_in(keys[8], 71), 0),
        "cap_values": gaussian(keys[6], (CLIPS, CAP, FEAT), 1.0, 6.0, ((0, 4), (1, 64))),
        "query_gain": jnp.clip(1.0 + 0.1 * jax.random.normal(keys[7], (FEAT,), jnp.float32), 0.5, 1.5),
    }


def block_grads(rows_q, rows_d, live_rows, keys_h, values_h, key_mask, gain_h):
    row_count = rows_q.shape[0]
    head_count, head_width = gain_h.shape
    scale = 1.0 / math.sqrt(head_width)
    inputs_f = rows_q.astype(jnp.float32).reshape(row_count, head_count, head_width)
    inv_rms = lax.rsqrt(lax.optimization_barrier(jnp.mean(inputs_f * inputs_f, axis=-1, keepdims=True)) + 1e-06)
    normed = inputs_f * inv_rms
    q_normed = (normed * gain_h).astype(jnp.bfloat16)
    live_grad = jnp.where(live_rows[:, None], rows_d, jnp.zeros_like(rows_d)).reshape(row_count, head_count, head_width)
    scores = jnp.einsum('thd,chd->htc', q_normed.astype(jnp.float32), keys_h.astype(jnp.float32)) * scale
    scores = jnp.where(key_mask, scores, -jnp.inf)
    highest = lax.optimization_barrier(jnp.max(scores, axis=-1, keepdims=True))
    expo = jnp.exp(scores - highest)
    probs = expo / lax.optimization_barrier(jnp.sum(expo, axis=-1, keepdims=True))
    probs_bf = probs.astype(jnp.bfloat16)
    dprobs = jnp.einsum('thd,chd->htc', live_grad.astype(jnp.float32), values_h.astype(jnp.float32))
    row_delta = lax.optimization_barrier(jnp.sum(probs * dprobs, axis=-1, keepdims=True))
    dscores = (probs * (dprobs - row_delta) * scale).astype(jnp.bfloat16)
    dnormed = jnp.einsum('htc,chd->thd', dscores.astype(jnp.float32), keys_h.astype(jnp.float32))
    key_term = jnp.einsum('htc,thd->chd', dscores.astype(jnp.float32), q_normed.astype(jnp.float32))
    value_term = jnp.einsum('htc,thd->chd', probs_bf.astype(jnp.float32), live_grad.astype(jnp.float32))
    gain_term = lax.optimization_barrier(jnp.sum(dnormed * normed, axis=0))
    scaled = gain_h * dnormed
    dinput = inv_rms * (scaled - normed * lax.optimization_barrier(jnp.mean(scaled * normed, axis=-1, keepdims=True)))
    return (dinput.astype(jnp.bfloat16).reshape(row_count, head_count * head_width), key_term, value_term, gain_term)

def reference(queries, grad_out, kept_pos, kept_count, caption_len, cap_keys, cap_values, query_gain):
    gain_h = query_gain.reshape(HEADS, HEAD_DIM)
    query_parts = []
    key_parts = []
    value_parts = []
    gain_total = jnp.zeros((HEADS, HEAD_DIM), jnp.float32)
    for clip_index in range(CLIPS):
        keys_h = cap_keys[clip_index].reshape(CAP, HEADS, HEAD_DIM)
        values_h = cap_values[clip_index].reshape(CAP, HEADS, HEAD_DIM)
        key_mask = jnp.arange(CAP) < caption_len[clip_index]

        def shard_step(carry_state, inputs):
            rows_q, rows_d, layout, count = inputs
            live_rows = jnp.arange(SHARD) < count
            dinput, key_term, value_term, gain_term = block_grads(rows_q, rows_d, live_rows, keys_h, values_h, key_mask, gain_h)
            placed = jnp.zeros((SHARD, FEAT), jnp.bfloat16).at[layout].set(dinput)
            return ((carry_state[0] + key_term, carry_state[1] + value_term, carry_state[2] + gain_term), placed)
        init = (jnp.zeros((CAP, HEADS, HEAD_DIM), jnp.float32), jnp.zeros((CAP, HEADS, HEAD_DIM), jnp.float32), jnp.zeros((HEADS, HEAD_DIM), jnp.float32))
        inputs = (queries[clip_index].reshape(N_SEQ, SHARD, FEAT), grad_out[clip_index].reshape(N_SEQ, SHARD, FEAT), kept_pos[clip_index].reshape(N_SEQ, SHARD), kept_count[clip_index])
        (key_sum, value_sum, gain_sum), placed = lax.scan(shard_step, init, inputs)
        query_parts.append(placed.reshape(TOKENS, FEAT))
        key_parts.append(key_sum.reshape(CAP, FEAT).astype(jnp.bfloat16))
        value_parts.append(value_sum.reshape(CAP, FEAT).astype(jnp.bfloat16))
        gain_total = gain_total + gain_sum
    return (jnp.stack(query_parts), jnp.stack(key_parts), jnp.stack(value_parts), gain_total.reshape(FEAT))
```

```python
import functools
import math

import jax
import jax.numpy as jnp
from jax import lax
from jax.experimental import pallas as pl
from jax.experimental.pallas import tpu as pltpu
from jax.sharding import Mesh, PartitionSpec as P

HEAD_DIM = 128
ROWS = 8
NZ, NY, NX = 8, 2, 4
SEQ = ("z", "yh", "x")
CHUNKS = (24,)
F32, BF16 = jnp.float32, jnp.bfloat16
NT = (((1,), (1,)), ((), ()))
TN = (((0,), (0,)), ((), ()))
NN = (((1,), (0,)), ((), ()))


def dot(a, b, dims):
    return lax.dot_general(a, b, dims, preferred_element_type=F32)


def send(value, axis, size, by):
    return lax.ppermute(value, axis, [(i, (i + by) % size) for i in range(size)])


UNIT = NY * ROWS
ZROWS = NX * UNIT
XROWS = NZ * UNIT
ZORDER = (0, 1, 2, 3, 5, 6, 7)


def kernel(first, *refs):
    (count_ref, q_ref, d_ref, gain_ref, pos_ref, bias_ref) = refs[:6]
    k_refs, v_refs = refs[6:15], refs[15:19]
    rest = refs[19 + (0 if first else 1):]
    qg_ref, dk_ref, dka_ref, dkb_ref, dv0_ref, dv1_ref, dv2_ref, dv3_ref, gg_ref, perm, bias = rest
    rows = q_ref.shape[0]
    count = count_ref[0]
    scale = 1.0 / math.sqrt(HEAD_DIM)

    @pl.when(pl.program_id(0) == 0)
    def _():
        place = lax.broadcasted_iota(jnp.int32, (rows, rows), 0)
        row = lax.broadcasted_iota(jnp.int32, (rows, rows), 1)
        hit = (place == pos_ref[...]) & (row < count)
        perm[...] = jnp.where(hit, 1.0, 0.0).astype(BF16)
        bias[...] = jnp.broadcast_to(bias_ref[...], bias.shape)

    gain = gain_ref[...]
    k = jnp.concatenate([r[...] for r in k_refs], axis=0)
    v_parts = [r[...] for r in v_refs]
    v = jnp.concatenate(
        [v_parts[dx][dz * UNIT : (dz + 1) * UNIT] for dz in range(NZ) for dx in range(NX)], axis=0
    )
    qf = q_ref[...].astype(F32)
    inv = lax.rsqrt(jnp.mean(qf * qf, axis=-1, keepdims=True) + 1e-6)
    normed = qf * inv
    qn = (normed * gain).astype(BF16)
    row = lax.broadcasted_iota(jnp.int32, (rows, HEAD_DIM), 0)
    live = jnp.where(row < count, d_ref[...].astype(F32), 0.0).astype(BF16)
    s = dot(k, qn, NT)
    wide = jnp.concatenate([bias[...]] * (rows // HEAD_DIM), axis=1)
    s = s * (scale * math.log2(math.e)) + wide
    e = jnp.exp2(s - jnp.max(s, axis=0, keepdims=True))
    p = e * (1.0 / jnp.sum(e, axis=0, keepdims=True))
    dp = dot(v, live, NT)
    delta = jnp.sum(p * dp, axis=0, keepdims=True)
    ds = (p * ((dp - delta) * scale)).astype(BF16)
    dk = dot(ds, qn, NN)
    dv = dot(p.astype(BF16), live, NN)
    dn = dot(k, ds, TN).T
    for n, dz in enumerate(ZORDER):
        dk_ref[n * ZROWS : (n + 1) * ZROWS] = dk[dz * ZROWS : (dz + 1) * ZROWS]
    half = ZROWS // 2
    dka_ref[...] = dk[4 * ZROWS : 4 * ZROWS + half].astype(BF16)
    dkb_ref[...] = dk[4 * ZROWS + half : 5 * ZROWS].astype(BF16)
    for dx, ref in enumerate((dv0_ref, dv1_ref, dv2_ref, dv3_ref)):
        for dz in range(NZ):
            at = dz * ZROWS + dx * UNIT
            ref[dz * UNIT : (dz + 1) * UNIT] = dv[at : at + UNIT].astype(ref.dtype)
    prod = dn * normed
    gg_ref[...] = jnp.sum(prod, axis=0, keepdims=True)[None]
    mean = jnp.mean(prod * gain, axis=-1, keepdims=True)
    dx_rows = inv * (gain * dn - normed * mean)
    qg_ref[...] = dot(perm[...], dx_rows.astype(BF16), NN).astype(BF16)


def grads(head, heads, count, q, d, gain, pos, bias, k_parts, v_parts, before):
    rows, feat = q.shape
    cols = heads * HEAD_DIM
    at = lambda i, *_: (0, head + i)
    here = lambda i, *_: (0, i)
    fixed = lambda i, *_: (0, 0)
    half = ZROWS // 2
    outs = [
        (rows, feat, BF16, at),
        (7 * ZROWS, cols, F32, here),
        (half, cols, BF16, here),
        (half, cols, BF16, here),
        (XROWS, cols, F32, here),
        (XROWS, cols, BF16, here),
        (XROWS, cols, BF16, here),
        (XROWS, cols, BF16, here),
    ]
    first = before is None
    in_specs = [
        pl.BlockSpec((rows, HEAD_DIM), at),
        pl.BlockSpec((rows, HEAD_DIM), at),
        pl.BlockSpec((1, HEAD_DIM), at),
        pl.BlockSpec(pos.shape, fixed),
        pl.BlockSpec(bias.shape, fixed),
    ] + [pl.BlockSpec((part.shape[0], HEAD_DIM), here) for part in k_parts + v_parts]
    args = [count, q, d, gain, pos, bias, *k_parts, *v_parts]
    aliases = {}
    if not first:
        in_specs.append(pl.BlockSpec(memory_space=pl.ANY))
        aliases = {len(args): 0}
        args.append(before)
    scores = heads * rows * bias.shape[0]
    return pl.pallas_call(
        functools.partial(kernel, first),
        grid_spec=pltpu.PrefetchScalarGridSpec(
            num_scalar_prefetch=1,
            grid=(heads,),
            in_specs=in_specs,
            out_specs=[pl.BlockSpec((r, HEAD_DIM), where) for r, _, _, where in outs]
            + [pl.BlockSpec((1, 1, HEAD_DIM), lambda i, *_: (i, 0, 0))],
            scratch_shapes=[
                pltpu.VMEM((rows, rows), BF16),
                pltpu.VMEM((bias.shape[0], HEAD_DIM), F32),
            ],
        ),
        out_shape=[jax.ShapeDtypeStruct((r, c), t) for r, c, t, _ in outs]
        + [jax.ShapeDtypeStruct((heads, 1, HEAD_DIM), F32)],
        input_output_aliases=aliases,
        compiler_params=pltpu.CompilerParams(vmem_limit_bytes=40 * 1024 * 1024),
        cost_estimate=pl.CostEstimate(
            flops=12 * scores * HEAD_DIM, bytes_accessed=20 * rows * cols, transcendentals=scores
        ),
        name="head_grads",
    )(*args)


def gather_keys(rows):
    half = ZROWS // 2
    parts = {0: rows}
    ahead = behind = rows
    for step in range(1, NZ // 2):
        ahead, behind = send(ahead, "z", NZ, 1), send(behind, "z", NZ, -1)
        parts[NZ - step], parts[step] = ahead, behind
    ahead, behind = send(ahead[:half], "z", NZ, 1), send(behind[half:], "z", NZ, -1)
    return [parts[dz] for dz in range(4)] + [ahead, behind] + [parts[dz] for dz in range(5, NZ)]


def gather_values(rows):
    return [rows] + [send(rows, "x", NX, -dx) for dx in range(1, NX)]


def sum_keys(terms, ahead, behind):
    half = ZROWS // 2
    term = lambda dz: terms[ZORDER.index(dz) * ZROWS : (ZORDER.index(dz) + 1) * ZROWS]
    wide = lambda part: part.astype(F32)
    ahead, behind = send(ahead, "z", NZ, 1), send(behind, "z", NZ, -1)
    three, five = term(3), term(5)
    ahead = jnp.concatenate([wide(ahead) + three[:half], three[half:]], axis=0)
    behind = jnp.concatenate([five[:half], wide(behind) + five[half:]], axis=0)
    for dz in (2, 1):
        ahead = send(ahead.astype(BF16), "z", NZ, 1)
        behind = send(behind.astype(BF16), "z", NZ, -1)
        ahead, behind = wide(ahead) + term(dz), wide(behind) + term(NZ - dz)
    ahead = send(ahead.astype(BF16), "z", NZ, 1)
    behind = send(behind.astype(BF16), "z", NZ, -1)
    total = term(0) + wide(ahead) + wide(behind)
    parts = [
        send(total[dx * UNIT : (dx + 1) * UNIT].astype(BF16), "x", NX, dx) for dx in range(1, NX)
    ]
    return total[:UNIT] + sum(wide(part) for part in parts)


def sum_values(own, others):
    parts = [send(part, "x", NX, dx + 1) for dx, part in enumerate(others)]
    total = own + sum(part.astype(F32) for part in parts)
    parts = [
        send(total[dz * UNIT : (dz + 1) * UNIT].astype(BF16), "z", NZ, dz) for dz in range(1, NZ)
    ]
    return total[:UNIT] + sum(part.astype(F32) for part in parts)


def sum_gain(gain):
    clips = lax.axis_size("clip")
    quarter = gain.shape[0] // clips
    mine = lax.axis_index("clip")
    pieces = [
        lax.dynamic_slice_in_dim(gain, ((mine + by) % clips) * quarter, quarter)
        for by in range(clips)
    ]
    total = pieces[0] + sum(send(pieces[by], "clip", clips, by) for by in range(1, clips))
    total = total + sum(send(total, "x", NX, by) for by in range(1, NX))
    for step in (1, 2, 4):
        total = total + lax.ppermute(total, "z", [(i, i ^ step) for i in range(NZ)])
    return total + send(total, "yh", NY, 1)


def body(queries, grad_out, kept_pos, kept_count, caption_len, cap_keys, cap_values, query_gain):
    z, yh, x = (lax.axis_index(name) for name in SEQ)
    feat = queries.shape[-1]
    cap = cap_keys.shape[1] * NZ * NY * NX
    count = lax.dynamic_slice_in_dim(kept_count[0], (z * NY + yh) * NX + x, 1)
    slot = jnp.arange(cap, dtype=jnp.int32)[:, None]
    at_z, at_x = (z + slot // ZROWS) % NZ, (x + slot // UNIT) % NX
    at_y = (yh + slot // ROWS) % NY
    caption = ((at_z * NY + at_y) * NX + at_x) * ROWS + slot % ROWS
    bias = jnp.where(caption < caption_len[0], 0.0, -jnp.inf).astype(F32)

    both = jnp.concatenate([cap_keys[0], cap_values[0]], axis=1)
    both = jnp.concatenate([both, send(both, "yh", NY, 1)], axis=0)
    keys, values = both[:, :feat], both[:, feat:]
    keys = jnp.concatenate([keys] + [send(keys, "x", NX, -dx) for dx in range(1, NX)], axis=0)
    values = jnp.concatenate([values] + [send(values, "z", NZ, -dz) for dz in range(1, NZ)], axis=0)

    gain_row = query_gain[None]
    query_grad = None
    key_sums, value_sums, gains = [], [], []
    head = 0
    for heads in CHUNKS:
        cols = slice(head * HEAD_DIM, (head + heads) * HEAD_DIM)
        k_parts, v_parts = gather_keys(keys[:, cols]), gather_values(values[:, cols])
        query_grad, dk, dka, dkb, dv0, dv1, dv2, dv3, gain = grads(
            head, heads, count, queries[0], grad_out[0], gain_row, kept_pos, bias, k_parts, v_parts,
            query_grad,
        )
        key_sums.append(sum_keys(dk, dka, dkb))
        value_sums.append(sum_values(dv0, (dv1, dv2, dv3)))
        gains.append(gain.reshape(-1))
        head += heads
    total = jnp.concatenate(key_sums + value_sums, axis=1)
    total = total[:ROWS] + send(total[ROWS:], "yh", NY, 1)
    total = total.astype(BF16)[None]
    gain_grad = sum_gain(jnp.concatenate(gains))
    return query_grad[None], total[..., :feat], total[..., feat:], gain_grad


def solution(mesh):
    parts = Mesh(mesh.devices.reshape(-1, NZ, NY, NX), ("clip",) + SEQ)
    return jax.shard_map(
        body,
        mesh=parts,
        in_specs=(
            P("clip", SEQ, None),
            P("clip", SEQ, None),
            P("clip", SEQ),
            P("clip", None),
            P("clip"),
            P("clip", SEQ, None),
            P("clip", SEQ, None),
            P(),
        ),
        out_specs=(P("clip", SEQ, None), P("clip", SEQ, None), P("clip", SEQ, None), P("clip")),
        check_vma=False,
    )
```

```python
import functools
import math

import jax
import jax.numpy as jnp
from jax import lax
from jax.experimental import pallas as pl
from jax.experimental.pallas import tpu as pltpu
from jax.sharding import Mesh, PartitionSpec as P

HEAD_DIM = 128
ROWS = 8
NZ, NY, NX = 8, 2, 4
SEQ = ("z", "yh", "x")
F32, BF16 = jnp.float32, jnp.bfloat16
NT = (((1,), (1,)), ((), ()))
TN = (((0,), (0,)), ((), ()))
NN = (((1,), (0,)), ((), ()))


def dot(a, b, dims):
    return lax.dot_general(a, b, dims, preferred_element_type=F32)


def send(value, axis, size, by):
    return lax.ppermute(value, axis, [(i, (i + by) % size) for i in range(size)])


NXY = NX * NY
ZROWS = NXY * ROWS
XROWS = NZ * ROWS
UNIT = NY * ROWS
PART = XROWS + ROWS
CHUNKS = (12, 12)
PACK = 2
FAR, HALF = NZ // 2, ZROWS // 2
EARLY = (FAR * ZROWS, FAR * ZROWS + HALF, FAR * ZROWS - HALF, (FAR + 1) * ZROWS)
KEPT = 2 + len(EARLY)


def two_terms(value, high):
    row = lax.broadcasted_iota(jnp.int32, (ROWS, value.shape[1]), 0)
    return jnp.where(row == 0, high, jnp.where(row == 1, value - high, 0.0))


def kernel(first, *refs):
    (scalar_ref, q_ref, d_ref, gain_ref, pos_ref, bias_ref, v_ref) = refs[:7]
    k_refs = refs[7:16]
    rest = refs[16 + (0 if first else KEPT):]
    qg_ref, dk_ref, *dk_refs, dv_ref, perm, bias = rest
    at_x = scalar_ref[1]
    rows = q_ref.shape[0]
    count = scalar_ref[0]
    scale = 1.0 / math.sqrt(HEAD_DIM)

    @pl.when(pl.program_id(0) == 0)
    def _():
        place = lax.broadcasted_iota(jnp.int32, (rows, rows), 0)
        row = lax.broadcasted_iota(jnp.int32, (rows, rows), 1)
        hit = (place == pos_ref[...]) & (row < count)
        perm[...] = jnp.where(hit, 1.0, 0.0).astype(BF16)
        bias[...] = jnp.broadcast_to(bias_ref[...], bias.shape)

    xs = [lax.rem(at_x + dx, NX) for dx in range(NX)]
    wide = NY * XROWS
    v = [v_ref[pl.ds(pl.multiple_of(x * wide, wide), wide)].astype(F32) for x in xs]
    v_all = jnp.concatenate(
        [
            v[dx][(y * NZ + dz) * ROWS : (y * NZ + dz + 1) * ROWS]
            for dz in range(NZ) for dx in range(NX) for y in range(NY)
        ],
        axis=0,
    ).astype(BF16)
    k_all = jnp.concatenate([r[...] for r in k_refs], axis=0)
    mask = jnp.concatenate([bias[...]] * (rows // HEAD_DIM), axis=1)
    row = lax.broadcasted_iota(jnp.int32, (rows, HEAD_DIM), 0)
    columns = [slice(n * HEAD_DIM, (n + 1) * HEAD_DIM) for n in range(PACK)]
    before = []
    for at in columns:
        gain, k, v = gain_ref[:, at], k_all[:, at], v_all[:, at]
        qf = q_ref[:, at].astype(F32)
        inv = lax.rsqrt(jnp.mean(qf * qf, axis=-1, keepdims=True) + 1e-6)
        normed = qf * inv
        qn = (normed * gain).astype(BF16)
        live = jnp.where(row < count, d_ref[:, at].astype(F32), 0.0).astype(BF16)
        before.append((gain, k, inv, normed, qn, live, dot(k, qn, NT), dot(v, live, NT)))
    between = []
    for *_, s, dp in before:
        s = s * (scale * math.log2(math.e)) + mask
        e = jnp.exp2(s - jnp.max(s, axis=0, keepdims=True))
        p = e * (1.0 / jnp.sum(e, axis=0, keepdims=True))
        delta = jnp.sum(p * dp, axis=0, keepdims=True)
        between.append((p.astype(BF16), (p * ((dp - delta) * scale)).astype(BF16)))
    dks, dvs, groups = [], [], []
    for at, (gain, k, inv, normed, qn, live, _, _), (p, ds) in zip(columns, before, between):
        dks.append(dot(ds, qn, NN))
        dvs.append(dot(p, live, NN))
        dn = dot(k, ds, TN).T
        prod = dn * normed
        total = jnp.sum(prod, axis=0, keepdims=True)
        groups.append(two_terms(total, total.astype(BF16).astype(F32)))
        mean = jnp.mean(prod * gain, axis=-1, keepdims=True)
        dx_rows = inv * (gain * dn - normed * mean)
        qg_ref[:, at] = dot(perm[...], dx_rows.astype(BF16), NN).astype(BF16)
    dk, dv, group = (jnp.concatenate(parts, axis=1) for parts in (dks, dvs, groups))
    dk_ref[...] = dk
    for ref, at in zip(dk_refs, EARLY):
        ref[...] = dk[at : at + HALF].astype(BF16)
    for dx, x in enumerate(xs):
        at = [[dz * ZROWS + (dx * NY + y) * ROWS for dz in range(NZ)] for y in range(NY)]
        part = jnp.concatenate([p for y in range(NY) for p in [dv[k : k + ROWS] for k in at[y]] + [group]], axis=0)
        dv_ref[pl.ds(pl.multiple_of(x * NY * PART, UNIT), NY * PART)] = part.astype(BF16)


def grads(head, heads, scalars, q, d, gain, pos, bias, v, k_parts, before):
    rows, feat = q.shape
    cap = bias.shape[0]
    cols = heads * HEAD_DIM
    at = lambda i, *_: (0, head // PACK + i)
    here = lambda i, *_: (0, i)
    fixed = lambda i, *_: (0, 0)
    outs = [
        (rows, feat, BF16, at),
        (cap, feat, F32, at),
        *[(HALF, feat, BF16, at)] * len(EARLY),
        (NXY * PART, cols, BF16, here),
    ]
    first = before is None
    in_specs = [
        pl.BlockSpec((rows, PACK * HEAD_DIM), at),
        pl.BlockSpec((rows, PACK * HEAD_DIM), at),
        pl.BlockSpec((1, PACK * HEAD_DIM), at),
        pl.BlockSpec(pos.shape, fixed),
        pl.BlockSpec(bias.shape, fixed),
        pl.BlockSpec((cap, PACK * HEAD_DIM), here),
    ] + [pl.BlockSpec((part.shape[0], PACK * HEAD_DIM), at) for part in k_parts]
    args = [scalars, q, d, gain, pos, bias, v, *k_parts]
    aliases = {}
    if not first:
        in_specs += [pl.BlockSpec(memory_space=pl.ANY)] * KEPT
        aliases = {len(args) + n: n for n in range(KEPT)}
        args += before
    scores = heads * rows * cap
    return pl.pallas_call(
        functools.partial(kernel, first),
        grid_spec=pltpu.PrefetchScalarGridSpec(
            num_scalar_prefetch=1,
            grid=(heads // PACK,),
            in_specs=in_specs,
            out_specs=[pl.BlockSpec((r, PACK * HEAD_DIM), where) for r, _, _, where in outs],
            scratch_shapes=[pltpu.VMEM((rows, rows), BF16), pltpu.VMEM((cap, HEAD_DIM), F32)],
        ),
        out_shape=[jax.ShapeDtypeStruct((r, c), t) for r, c, t, _ in outs],
        input_output_aliases=aliases,
        compiler_params=pltpu.CompilerParams(vmem_limit_bytes=60 * 1024 * 1024),
        cost_estimate=pl.CostEstimate(
            flops=12 * scores * HEAD_DIM, bytes_accessed=heads * 5_500_000, transcendentals=scores
        ),
        name="head_grads",
    )(*args)


def exchange(blocks, axes):
    return lax.all_to_all(blocks, axes, 0, 0, tiled=True)


def spread(rows, axes, count):
    return exchange(jnp.broadcast_to(rows[None], (count, *rows.shape)), axes).reshape(-1, rows.shape[1])


def add_up(rows, count):
    blocks = rows.reshape(count, rows.shape[0] // count, rows.shape[1])
    return sum(blocks[i].astype(F32) for i in range(count))


def roll_rows(value, start):
    return lax.dynamic_slice_in_dim(jnp.concatenate([value, value], axis=0), start, value.shape[0])


def both_ways(ahead, behind):
    return send(ahead, "z", NZ, 1), send(behind, "z", NZ, -1)


def gather(cap_keys, cap_values):
    yh = lax.axis_index("yh")
    other = send(cap_keys, "yh", NY, 1)
    keys = [jnp.where(yh == y, cap_keys, other) for y in range(NY)]
    keys = jnp.concatenate(keys, axis=0)
    keys = jnp.concatenate([keys] + [send(keys, "x", NX, -dx) for dx in range(1, NX)], axis=0)
    values = spread(cap_values, "z", NZ)
    values = roll_rows(values, lax.axis_index("z") * ROWS)
    parts = {0: keys}
    ahead = behind = keys
    for step in range(1, FAR):
        ahead, behind = both_ways(ahead, behind)
        parts[NZ - step], parts[step] = ahead, behind
    ahead, behind = both_ways(ahead[:HALF], behind[HALF:])
    pieces = [parts[dz] for dz in range(FAR)] + [ahead, behind] + [parts[dz] for dz in range(FAR + 1, NZ)]
    return pieces, values


def scatter(terms, far_a, far_b, three_b, five_a, value_parts, dv):
    term = lambda dz: terms[dz * ZROWS : (dz + 1) * ZROWS]
    wide = lambda part: part.astype(F32)
    tie = lax.optimization_barrier
    ahead, behind = both_ways(far_a, far_b)
    ahead, behind, first = tie((ahead, behind, value_parts))
    second = exchange(dv, ("x", "yh"))
    ahead = (wide(ahead) + term(FAR - 1)[:HALF]).astype(BF16)
    behind = (wide(behind) + term(FAR + 1)[HALF:]).astype(BF16)
    ahead, behind = both_ways(
        jnp.concatenate([ahead, three_b], axis=0), jnp.concatenate([five_a, behind], axis=0)
    )
    ahead, behind = both_ways(
        (wide(ahead) + term(2)).astype(BF16), (wide(behind) + term(NZ - 2)).astype(BF16)
    )
    ahead, behind, second = tie((ahead, behind, second))
    ahead, behind = both_ways(
        (wide(ahead) + term(1)).astype(BF16), (wide(behind) + term(NZ - 1)).astype(BF16)
    )
    value_sum = jnp.concatenate([add_up(first, NXY), add_up(second, NXY)], axis=1)
    gain = value_sum[XROWS : XROWS + 1] + value_sum[XROWS + 1 : XROWS + 2]
    gain = two_terms(gain, lax.reduce_precision(gain, 8, 7))
    value_sum = roll_rows(value_sum[:XROWS], (NZ - lax.axis_index("z")) % NZ * ROWS)
    value_sum = value_sum.reshape(NZ, ROWS, -1)
    blocks = jnp.concatenate([value_sum, jnp.broadcast_to(gain[None], value_sum.shape)], axis=1)
    blocks = blocks.astype(BF16).reshape(2 * XROWS, -1)
    value_grad = add_up(exchange(blocks, "z"), NZ)
    key_sum = term(0) + wide(ahead) + wide(behind)
    parts = [
        send(key_sum[dx * UNIT : (dx + 1) * UNIT].astype(BF16), "x", NX, dx) for dx in range(1, NX)
    ]
    key_sum = roll_rows(key_sum[:UNIT] + sum(wide(part) for part in parts), lax.axis_index("yh") * ROWS)
    key_grad = key_sum[:ROWS] + send(key_sum[ROWS:], "yh", NY, 1)
    clips, mine = lax.axis_size("clip"), lax.axis_index("clip")
    gain = value_grad[ROWS : ROWS + 1] + value_grad[ROWS + 1 : ROWS + 2]
    gain = roll_rows(gain.reshape(clips, -1), mine)
    gain = gain[:1] + sum(send(gain[by : by + 1], "clip", clips, by) for by in range(1, clips))
    return key_grad, value_grad[:ROWS], gain[0]


def body(queries, grad_out, kept_pos, kept_count, caption_len, cap_keys, cap_values, query_gain):
    z, yh, x = (lax.axis_index(name) for name in SEQ)
    feat = queries.shape[-1]
    cap = cap_keys.shape[1] * NZ * NY * NX
    count = lax.dynamic_index_in_dim(kept_count[0], (z * NY + yh) * NX + x, keepdims=False)
    scalars = jnp.stack([count, x])
    slot = jnp.arange(cap, dtype=jnp.int32)[:, None]
    at_z, at_x, at_y = (z + slot // ZROWS) % NZ, (x + slot // UNIT) % NX, slot // ROWS % NY
    caption = ((at_z * NY + at_y) * NX + at_x) * ROWS + slot % ROWS
    bias = jnp.where(caption < caption_len[0], 0.0, -jnp.inf).astype(F32)
    key_parts, values = gather(cap_keys[0], cap_values[0])
    run = lambda head, heads, v, before: grads(
        head, heads, scalars, queries[0], grad_out[0], query_gain[None], kept_pos, bias, v, key_parts,
        before,
    )
    split = CHUNKS[0] * HEAD_DIM
    v1, v2 = (spread(part, ("x", "yh"), NXY) for part in (values[:, :split], values[:, split:]))
    *kept, dv1 = run(0, CHUNKS[0], v1, None)
    *kept, dv1, v2 = lax.optimization_barrier((*kept, dv1, v2))
    *kept, dv2 = run(CHUNKS[0], CHUNKS[1], v2, kept)
    query_grad, *terms = kept
    key_grad, value_grad, gain_grad = scatter(*terms, exchange(dv1, ("x", "yh")), dv2)
    return query_grad[None], key_grad.astype(BF16)[None], value_grad.astype(BF16)[None], gain_grad


def solution(mesh):
    parts = Mesh(mesh.devices.reshape(-1, NZ, NY, NX), ("clip",) + SEQ)
    return jax.shard_map(
        body,
        mesh=parts,
        in_specs=(
            P("clip", SEQ, None),
            P("clip", SEQ, None),
            P("clip", SEQ),
            P("clip", None),
            P("clip"),
            P("clip", SEQ, None),
            P("clip", SEQ, None),
            P(),
        ),
        out_specs=(P("clip", SEQ, None), P("clip", SEQ, None), P("clip", SEQ, None), P("clip")),
        check_vma=False,
    )
```

```python
import functools
import math

import jax
import jax.numpy as jnp
from jax import lax
from jax.experimental import pallas as pl
from jax.experimental.pallas import tpu as pltpu
from jax.sharding import Mesh, PartitionSpec as P

HEAD_DIM = 128
ROWS = 8
NZ, NY, NX = 8, 2, 4
SEQ = ("z", "yh", "x")
F32, BF16 = jnp.float32, jnp.bfloat16
NT = (((1,), (1,)), ((), ()))
TN = (((0,), (0,)), ((), ()))
NN = (((1,), (0,)), ((), ()))


def dot(a, b, dims):
    return lax.dot_general(a, b, dims, preferred_element_type=F32)


def send(value, axis, size, by):
    return lax.ppermute(value, axis, [(i, (i + by) % size) for i in range(size)])


NXY = NX * NY
ZROWS = NXY * ROWS
XROWS = NZ * ROWS
UNIT = NY * ROWS
PART = XROWS + ROWS
CHUNKS = (12, 12)
PACK = 2
FAR, HALF = NZ // 2, ZROWS // 2
EARLY = (FAR - 1, FAR + 1)
KEPT = 2 + len(EARLY)


def two_terms(value, high):
    row = lax.broadcasted_iota(jnp.int32, (ROWS, value.shape[1]), 0)
    return jnp.where(row == 0, high, jnp.where(row == 1, value - high, 0.0))


def kernel(first, *refs):
    (scalar_ref, q_ref, d_ref, gain_ref, pos_ref, bias_ref, v_ref) = refs[:7]
    k_refs = refs[7:16]
    rest = refs[16 + (0 if first else KEPT):]
    qg_ref, dk_ref, three_ref, five_ref, far_ref, dv_ref, perm, bias = rest
    at_x = scalar_ref[1]
    rows = q_ref.shape[0]
    count = scalar_ref[0]
    scale = 1.0 / math.sqrt(HEAD_DIM)

    @pl.when(pl.program_id(0) == 0)
    def _():
        place = lax.broadcasted_iota(jnp.int32, (rows, rows), 0)
        row = lax.broadcasted_iota(jnp.int32, (rows, rows), 1)
        hit = (place == pos_ref[...]) & (row < count)
        perm[...] = jnp.where(hit, 1.0, 0.0).astype(BF16)
        bias[...] = jnp.broadcast_to(bias_ref[...], bias.shape)

    xs = [lax.rem(at_x + dx, NX) for dx in range(NX)]
    wide = NY * XROWS
    v = [v_ref[pl.ds(pl.multiple_of(x * wide, wide), wide)].astype(F32) for x in xs]
    v_all = jnp.concatenate(
        [
            v[dx][(y * NZ + dz) * ROWS : (y * NZ + dz + 1) * ROWS]
            for dz in range(NZ) for dx in range(NX) for y in range(NY)
        ],
        axis=0,
    ).astype(BF16)
    k_all = jnp.concatenate([r[...] for r in k_refs], axis=0)
    mask = jnp.concatenate([bias[...]] * (rows // HEAD_DIM), axis=1)
    row = lax.broadcasted_iota(jnp.int32, (rows, HEAD_DIM), 0)
    columns = [slice(n * HEAD_DIM, (n + 1) * HEAD_DIM) for n in range(PACK)]
    before = []
    for at in columns:
        gain, k, v = gain_ref[:, at], k_all[:, at], v_all[:, at]
        qf = q_ref[:, at].astype(F32)
        inv = lax.rsqrt(jnp.mean(qf * qf, axis=-1, keepdims=True) + 1e-6)
        normed = qf * inv
        qn = (normed * gain).astype(BF16)
        live = jnp.where(row < count, d_ref[:, at].astype(F32), 0.0).astype(BF16)
        before.append((gain, k, inv, normed, qn, live, dot(k, qn, NT), dot(v, live, NT)))
    between = []
    for *_, s, dp in before:
        s = s * (scale * math.log2(math.e)) + mask
        e = jnp.exp2(s - jnp.max(s, axis=0, keepdims=True))
        p = e * (1.0 / jnp.sum(e, axis=0, keepdims=True))
        delta = jnp.sum(p * dp, axis=0, keepdims=True)
        between.append((p.astype(BF16), (p * ((dp - delta) * scale)).astype(BF16)))
    dks, dvs, groups = [], [], []
    for at, (gain, k, inv, normed, qn, live, _, _), (p, ds) in zip(columns, before, between):
        dks.append(dot(ds, qn, NN))
        dvs.append(dot(p, live, NN))
        dn = dot(k, ds, TN).T
        prod = dn * normed
        total = jnp.sum(prod, axis=0, keepdims=True)
        groups.append(two_terms(total, total.astype(BF16).astype(F32)))
        mean = jnp.mean(prod * gain, axis=-1, keepdims=True)
        dx_rows = inv * (gain * dn - normed * mean)
        qg_ref[:, at] = dot(perm[...], dx_rows.astype(BF16), NN).astype(BF16)
    dk, dv, group = (jnp.concatenate(parts, axis=1) for parts in (dks, dvs, groups))
    dk_ref[...] = dk
    for ref, dz in zip((three_ref, five_ref, far_ref), (*EARLY, FAR)):
        ref[...] = dk[dz * ZROWS : (dz + 1) * ZROWS].astype(BF16)
    for dx, x in enumerate(xs):
        at = [[dz * ZROWS + (dx * NY + y) * ROWS for dz in range(NZ)] for y in range(NY)]
        part = jnp.concatenate([p for y in range(NY) for p in [dv[k : k + ROWS] for k in at[y]] + [group]], axis=0)
        dv_ref[pl.ds(pl.multiple_of(x * NY * PART, UNIT), NY * PART)] = part.astype(BF16)


def grads(head, heads, scalars, q, d, gain, pos, bias, v, k_parts, before):
    rows, feat = q.shape
    cap = bias.shape[0]
    cols = heads * HEAD_DIM
    at = lambda i, *_: (0, head // PACK + i)
    here = lambda i, *_: (0, i)
    fixed = lambda i, *_: (0, 0)
    outs = [
        (rows, feat, BF16, at),
        (cap, feat, F32, at),
        *[(ZROWS, feat, BF16, at)] * len(EARLY),
        (ZROWS, cols, BF16, here),
        (NXY * PART, cols, BF16, here),
    ]
    first = before is None
    in_specs = [
        pl.BlockSpec((rows, PACK * HEAD_DIM), at),
        pl.BlockSpec((rows, PACK * HEAD_DIM), at),
        pl.BlockSpec((1, PACK * HEAD_DIM), at),
        pl.BlockSpec(pos.shape, fixed),
        pl.BlockSpec(bias.shape, fixed),
        pl.BlockSpec((cap, PACK * HEAD_DIM), here),
    ] + [pl.BlockSpec((part.shape[0], PACK * HEAD_DIM), at) for part in k_parts]
    args = [scalars, q, d, gain, pos, bias, v, *k_parts]
    aliases = {}
    if not first:
        in_specs += [pl.BlockSpec(memory_space=pl.ANY)] * KEPT
        aliases = {len(args) + n: n for n in range(KEPT)}
        args += before
    scores = heads * rows * cap
    return pl.pallas_call(
        functools.partial(kernel, first),
        grid_spec=pltpu.PrefetchScalarGridSpec(
            num_scalar_prefetch=1,
            grid=(heads // PACK,),
            in_specs=in_specs,
            out_specs=[pl.BlockSpec((r, PACK * HEAD_DIM), where) for r, _, _, where in outs],
            scratch_shapes=[pltpu.VMEM((rows, rows), BF16), pltpu.VMEM((cap, HEAD_DIM), F32)],
        ),
        out_shape=[jax.ShapeDtypeStruct((r, c), t) for r, c, t, _ in outs],
        input_output_aliases=aliases,
        compiler_params=pltpu.CompilerParams(vmem_limit_bytes=60 * 1024 * 1024),
        cost_estimate=pl.CostEstimate(
            flops=12 * scores * HEAD_DIM, bytes_accessed=heads * 5_500_000, transcendentals=scores
        ),
        name="head_grads",
    )(*args)


def exchange(blocks, axes):
    return lax.all_to_all(blocks, axes, 0, 0, tiled=True)


def spread(rows, axes, count):
    return exchange(jnp.broadcast_to(rows[None], (count, *rows.shape)), axes).reshape(-1, rows.shape[1])


def add_up(rows, count):
    blocks = rows.reshape(count, rows.shape[0] // count, rows.shape[1])
    return sum(blocks[i].astype(F32) for i in range(count))


def roll_rows(value, start):
    return lax.dynamic_slice_in_dim(jnp.concatenate([value, value], axis=0), start, value.shape[0])


def both_ways(ahead, behind):
    return send(ahead, "z", NZ, 1), send(behind, "z", NZ, -1)


def gather(cap_keys, cap_values):
    yh = lax.axis_index("yh")
    other = send(cap_keys, "yh", NY, 1)
    keys = [jnp.where(yh == y, cap_keys, other) for y in range(NY)]
    keys = jnp.concatenate(keys, axis=0)
    keys = jnp.concatenate([keys] + [send(keys, "x", NX, -dx) for dx in range(1, NX)], axis=0)
    values = spread(cap_values, "z", NZ)
    values = roll_rows(values, lax.axis_index("z") * ROWS)
    parts = {0: keys}
    ahead = behind = keys
    for step in range(1, FAR):
        ahead, behind = both_ways(ahead, behind)
        parts[NZ - step], parts[step] = ahead, behind
    ahead, behind = both_ways(ahead[:HALF], behind[HALF:])
    pieces = [parts[dz] for dz in range(FAR)] + [ahead, behind] + [parts[dz] for dz in range(FAR + 1, NZ)]
    return pieces, values


def scatter(terms, three, five, far, first, dv):
    term = lambda dz: terms[dz * ZROWS : (dz + 1) * ZROWS]
    wide = lambda part: part.astype(F32)
    far_got, far = far[0], send(far[1], "z", NZ, FAR)
    second = exchange(dv, ("x", "yh"))
    ahead, behind = both_ways(three, five)
    ahead, behind = both_ways(
        (wide(ahead) + term(2)).astype(BF16), (wide(behind) + term(NZ - 2)).astype(BF16)
    )
    ahead, behind, second = lax.optimization_barrier((ahead, behind, second))
    ahead, behind = both_ways(
        (wide(ahead) + term(1)).astype(BF16), (wide(behind) + term(NZ - 1)).astype(BF16)
    )
    value_sum = jnp.concatenate([add_up(first, NXY), add_up(second, NXY)], axis=1)
    gain = value_sum[XROWS : XROWS + 1] + value_sum[XROWS + 1 : XROWS + 2]
    gain = two_terms(gain, lax.reduce_precision(gain, 8, 7))
    value_sum = roll_rows(value_sum[:XROWS], (NZ - lax.axis_index("z")) % NZ * ROWS)
    value_sum = value_sum.reshape(NZ, ROWS, -1)
    blocks = jnp.concatenate([value_sum, jnp.broadcast_to(gain[None], value_sum.shape)], axis=1)
    blocks = blocks.astype(BF16).reshape(2 * XROWS, -1)
    value_grad = add_up(exchange(blocks, "z"), NZ)
    key_sum = term(0) + wide(ahead) + wide(behind) + wide(jnp.concatenate([far_got, far], axis=1))
    parts = [
        send(key_sum[dx * UNIT : (dx + 1) * UNIT].astype(BF16), "x", NX, dx) for dx in range(1, NX)
    ]
    key_sum = roll_rows(key_sum[:UNIT] + sum(wide(part) for part in parts), lax.axis_index("yh") * ROWS)
    key_grad = key_sum[:ROWS] + send(key_sum[ROWS:], "yh", NY, 1)
    clips, mine = lax.axis_size("clip"), lax.axis_index("clip")
    gain = value_grad[ROWS : ROWS + 1] + value_grad[ROWS + 1 : ROWS + 2]
    gain = roll_rows(gain.reshape(clips, -1), mine)
    gain = gain[:1] + sum(send(gain[by : by + 1], "clip", clips, by) for by in range(1, clips))
    return key_grad, value_grad[:ROWS], gain[0]


def body(queries, grad_out, kept_pos, kept_count, caption_len, cap_keys, cap_values, query_gain):
    z, yh, x = (lax.axis_index(name) for name in SEQ)
    feat = queries.shape[-1]
    cap = cap_keys.shape[1] * NZ * NY * NX
    count = lax.dynamic_index_in_dim(kept_count[0], (z * NY + yh) * NX + x, keepdims=False)
    scalars = jnp.stack([count, x])
    slot = jnp.arange(cap, dtype=jnp.int32)[:, None]
    at_z, at_x, at_y = (z + slot // ZROWS) % NZ, (x + slot // UNIT) % NX, slot // ROWS % NY
    caption = ((at_z * NY + at_y) * NX + at_x) * ROWS + slot % ROWS
    bias = jnp.where(caption < caption_len[0], 0.0, -jnp.inf).astype(F32)
    key_parts, values = gather(cap_keys[0], cap_values[0])
    run = lambda head, heads, v, before: grads(
        head, heads, scalars, queries[0], grad_out[0], query_gain[None], kept_pos, bias, v, key_parts,
        before,
    )
    split = CHUNKS[0] * HEAD_DIM
    v1, v2 = (spread(part, ("x", "yh"), NXY) for part in (values[:, :split], values[:, split:]))
    *kept, far1, dv1 = run(0, CHUNKS[0], v1, None)
    *kept, far1, dv1, v2 = lax.optimization_barrier((*kept, far1, dv1, v2))
    *kept, far2, dv2 = run(CHUNKS[0], CHUNKS[1], v2, kept)
    dv1, far1 = exchange(dv1, ("x", "yh")), send(far1, "z", NZ, FAR)
    *kept, far2, dv2, dv1, far1 = lax.optimization_barrier((*kept, far2, dv2, dv1, far1))
    query_grad, *terms = kept
    key_grad, value_grad, gain_grad = scatter(*terms, (far1, far2), dv1, dv2)
    return query_grad[None], key_grad.astype(BF16)[None], value_grad.astype(BF16)[None], gain_grad


def solution(mesh):
    parts = Mesh(mesh.devices.reshape(-1, NZ, NY, NX), ("clip",) + SEQ)
    return jax.shard_map(
        body,
        mesh=parts,
        in_specs=(
            P("clip", SEQ, None),
            P("clip", SEQ, None),
            P("clip", SEQ),
            P("clip", None),
            P("clip"),
            P("clip", SEQ, None),
            P("clip", SEQ, None),
            P(),
        ),
        out_specs=(P("clip", SEQ, None), P("clip", SEQ, None), P("clip", SEQ, None), P("clip")),
        check_vma=False,
    )
```

```python
import functools
import math

import jax
import jax.numpy as jnp
from jax import lax
from jax.experimental import pallas as pl
from jax.experimental.pallas import tpu as pltpu
from jax.sharding import Mesh, PartitionSpec as P

HEAD_DIM = 128
ROWS = 8
NZ, NY, NX = 8, 2, 4
SEQ = ("z", "yh", "x")
F32, BF16 = jnp.float32, jnp.bfloat16
NT = (((1,), (1,)), ((), ()))
TN = (((0,), (0,)), ((), ()))
NN = (((1,), (0,)), ((), ()))


def dot(a, b, dims):
    return lax.dot_general(a, b, dims, preferred_element_type=F32)


def send(value, axis, size, by):
    return lax.ppermute(value, axis, [(i, (i + by) % size) for i in range(size)])


NXY = NX * NY
ZROWS = NXY * ROWS
XROWS = NZ * ROWS
UNIT = NY * ROWS
PART = XROWS + ROWS
CHUNKS = (12, 12)
PACK = 2
FAR, HALF = NZ // 2, ZROWS // 2
EARLY = (FAR - 1, FAR + 1)
KEPT = 2 + len(EARLY)


def two_terms(value, high):
    row = lax.broadcasted_iota(jnp.int32, (ROWS, value.shape[1]), 0)
    return jnp.where(row == 0, high, jnp.where(row == 1, value - high, 0.0))


def kernel(first, *refs):
    (scalar_ref, q_ref, d_ref, gain_ref, pos_ref, bias_ref, v_ref) = refs[:7]
    k_refs = refs[7:16]
    rest = refs[16 + (0 if first else KEPT):]
    qg_ref, dk_ref, three_ref, five_ref, far_ref, dv_ref, perm, bias = rest
    at_x = scalar_ref[1]
    rows = q_ref.shape[0]
    count = scalar_ref[0]
    scale = 1.0 / math.sqrt(HEAD_DIM)

    @pl.when(pl.program_id(0) == 0)
    def _():
        place = lax.broadcasted_iota(jnp.int32, (rows, rows), 0)
        row = lax.broadcasted_iota(jnp.int32, (rows, rows), 1)
        hit = (place == pos_ref[...]) & (row < count)
        perm[...] = jnp.where(hit, 1.0, 0.0).astype(BF16)
        bias[...] = jnp.broadcast_to(bias_ref[...], bias.shape)

    xs = [lax.rem(at_x + dx, NX) for dx in range(NX)]
    wide = NY * XROWS
    v = [v_ref[pl.ds(pl.multiple_of(x * wide, wide), wide)].astype(F32) for x in xs]
    v_all = jnp.concatenate(
        [
            v[dx][(y * NZ + dz) * ROWS : (y * NZ + dz + 1) * ROWS]
            for dz in range(NZ) for dx in range(NX) for y in range(NY)
        ],
        axis=0,
    ).astype(BF16)
    k_all = jnp.concatenate([r[...] for r in k_refs], axis=0)
    mask = jnp.concatenate([bias[...]] * (rows // HEAD_DIM), axis=1)
    row = lax.broadcasted_iota(jnp.int32, (rows, HEAD_DIM), 0)
    columns = [slice(n * HEAD_DIM, (n + 1) * HEAD_DIM) for n in range(PACK)]
    before = []
    for at in columns:
        gain, k, v = gain_ref[:, at], k_all[:, at], v_all[:, at]
        qf = q_ref[:, at].astype(F32)
        inv = lax.rsqrt(jnp.mean(qf * qf, axis=-1, keepdims=True) + 1e-6)
        normed = qf * inv
        qn = (normed * gain).astype(BF16)
        live = jnp.where(row < count, d_ref[:, at].astype(F32), 0.0).astype(BF16)
        before.append((gain, k, inv, normed, qn, live, dot(k, qn, NT), dot(v, live, NT)))
    between = []
    for *_, s, dp in before:
        s = s * (scale * math.log2(math.e)) + mask
        e = jnp.exp2(s - jnp.max(s, axis=0, keepdims=True))
        p = e * (1.0 / jnp.sum(e, axis=0, keepdims=True))
        delta = jnp.sum(p * dp, axis=0, keepdims=True)
        between.append((p.astype(BF16), (p * ((dp - delta) * scale)).astype(BF16)))
    dks, dvs, groups = [], [], []
    for at, (gain, k, inv, normed, qn, live, _, _), (p, ds) in zip(columns, before, between):
        dks.append(dot(ds, qn, NN))
        dvs.append(dot(p, live, NN))
        dn = dot(k, ds, TN).T
        prod = dn * normed
        total = jnp.sum(prod, axis=0, keepdims=True)
        groups.append(two_terms(total, total.astype(BF16).astype(F32)))
        mean = jnp.mean(prod * gain, axis=-1, keepdims=True)
        dx_rows = inv * (gain * dn - normed * mean)
        qg_ref[:, at] = dot(perm[...], dx_rows.astype(BF16), NN).astype(BF16)
    dk, dv, group = (jnp.concatenate(parts, axis=1) for parts in (dks, dvs, groups))
    dk_ref[...] = dk
    for ref, dz in zip((three_ref, five_ref, far_ref), (*EARLY, FAR)):
        ref[...] = dk[dz * ZROWS : (dz + 1) * ZROWS].astype(BF16)
    for dx, x in enumerate(xs):
        at = [[dz * ZROWS + (dx * NY + y) * ROWS for dz in range(NZ)] for y in range(NY)]
        part = jnp.concatenate([p for y in range(NY) for p in [dv[k : k + ROWS] for k in at[y]] + [group]], axis=0)
        dv_ref[pl.ds(pl.multiple_of(x * NY * PART, UNIT), NY * PART)] = part.astype(BF16)


def grads(head, heads, scalars, q, d, gain, pos, bias, v, k_parts, before):
    rows, feat = q.shape
    cap = bias.shape[0]
    cols = heads * HEAD_DIM
    at = lambda i, *_: (0, head // PACK + i)
    here = lambda i, *_: (0, i)
    fixed = lambda i, *_: (0, 0)
    outs = [
        (rows, feat, BF16, at),
        (cap, feat, F32, at),
        *[(ZROWS, feat, BF16, at)] * len(EARLY),
        (ZROWS, cols, BF16, here),
        (NXY * PART, cols, BF16, here),
    ]
    first = before is None
    in_specs = [
        pl.BlockSpec((rows, PACK * HEAD_DIM), at),
        pl.BlockSpec((rows, PACK * HEAD_DIM), at),
        pl.BlockSpec((1, PACK * HEAD_DIM), at),
        pl.BlockSpec(pos.shape, fixed),
        pl.BlockSpec(bias.shape, fixed),
        pl.BlockSpec((cap, PACK * HEAD_DIM), at),
    ] + [pl.BlockSpec((part.shape[0], PACK * HEAD_DIM), at) for part in k_parts]
    args = [scalars, q, d, gain, pos, bias, v, *k_parts]
    aliases = {}
    if not first:
        in_specs += [pl.BlockSpec(memory_space=pl.ANY)] * KEPT
        aliases = {len(args) + n: n for n in range(KEPT)}
        args += before
    scores = heads * rows * cap
    return pl.pallas_call(
        functools.partial(kernel, first),
        grid_spec=pltpu.PrefetchScalarGridSpec(
            num_scalar_prefetch=1,
            grid=(heads // PACK,),
            in_specs=in_specs,
            out_specs=[pl.BlockSpec((r, PACK * HEAD_DIM), where) for r, _, _, where in outs],
            scratch_shapes=[pltpu.VMEM((rows, rows), BF16), pltpu.VMEM((cap, HEAD_DIM), F32)],
        ),
        out_shape=[jax.ShapeDtypeStruct((r, c), t) for r, c, t, _ in outs],
        input_output_aliases=aliases,
        compiler_params=pltpu.CompilerParams(vmem_limit_bytes=60 * 1024 * 1024),
        cost_estimate=pl.CostEstimate(
            flops=12 * scores * HEAD_DIM, bytes_accessed=heads * 5_500_000, transcendentals=scores
        ),
        name="head_grads",
    )(*args)


def exchange(blocks, axes):
    return lax.all_to_all(blocks, axes, 0, 0, tiled=True)


def spread(rows, axes, count):
    return exchange(jnp.broadcast_to(rows[None], (count, *rows.shape)), axes).reshape(-1, rows.shape[1])


def add_up(rows, count):
    blocks = rows.reshape(count, rows.shape[0] // count, rows.shape[1])
    return sum(blocks[i].astype(F32) for i in range(count))


def roll_rows(value, start):
    return lax.dynamic_slice_in_dim(jnp.concatenate([value, value], axis=0), start, value.shape[0])


def both_ways(ahead, behind):
    return send(ahead, "z", NZ, 1), send(behind, "z", NZ, -1)


def gather(cap_keys, cap_values):
    yh = lax.axis_index("yh")
    other = send(cap_keys, "yh", NY, 1)
    keys = [jnp.where(yh == y, cap_keys, other) for y in range(NY)]
    keys = jnp.concatenate(keys, axis=0)
    keys = jnp.concatenate([keys] + [send(keys, "x", NX, -dx) for dx in range(1, NX)], axis=0)
    values = spread(cap_values, "z", NZ)
    values = roll_rows(values, lax.axis_index("z") * ROWS)
    parts = {0: keys}
    ahead = behind = keys
    for step in range(1, FAR):
        ahead, behind = both_ways(ahead, behind)
        parts[NZ - step], parts[step] = ahead, behind
    ahead, behind = both_ways(ahead[:HALF], behind[HALF:])
    pieces = [parts[dz] for dz in range(FAR)] + [ahead, behind] + [parts[dz] for dz in range(FAR + 1, NZ)]
    return pieces, values


def scatter(terms, three, five, far, first, dv):
    term = lambda dz: terms[dz * ZROWS : (dz + 1) * ZROWS]
    wide = lambda part: part.astype(F32)
    far_got, far = far[0], send(far[1], "z", NZ, FAR)
    second = exchange(dv, ("x", "yh"))
    ahead, behind = both_ways(three, five)
    ahead, behind = both_ways(
        (wide(ahead) + term(2)).astype(BF16), (wide(behind) + term(NZ - 2)).astype(BF16)
    )
    ahead, behind, second = lax.optimization_barrier((ahead, behind, second))
    ahead, behind = both_ways(
        (wide(ahead) + term(1)).astype(BF16), (wide(behind) + term(NZ - 1)).astype(BF16)
    )
    value_sum = jnp.concatenate([add_up(first, NXY), add_up(second, NXY)], axis=1)
    gain = value_sum[XROWS : XROWS + 1] + value_sum[XROWS + 1 : XROWS + 2]
    gain = two_terms(gain, lax.reduce_precision(gain, 8, 7))
    value_sum = roll_rows(value_sum[:XROWS], (NZ - lax.axis_index("z")) % NZ * ROWS)
    value_sum = value_sum.reshape(NZ, ROWS, -1)
    blocks = jnp.concatenate([value_sum, jnp.broadcast_to(gain[None], value_sum.shape)], axis=1)
    blocks = blocks.astype(BF16).reshape(2 * XROWS, -1)
    value_grad = add_up(exchange(blocks, "z"), NZ)
    key_sum = term(0) + wide(ahead) + wide(behind) + wide(jnp.concatenate([far_got, far], axis=1))
    parts = [
        send(key_sum[dx * UNIT : (dx + 1) * UNIT].astype(BF16), "x", NX, dx) for dx in range(1, NX)
    ]
    key_sum = roll_rows(key_sum[:UNIT] + sum(wide(part) for part in parts), lax.axis_index("yh") * ROWS)
    key_grad = key_sum[:ROWS] + send(key_sum[ROWS:], "yh", NY, 1)
    clips, mine = lax.axis_size("clip"), lax.axis_index("clip")
    gain = value_grad[ROWS : ROWS + 1] + value_grad[ROWS + 1 : ROWS + 2]
    gain = roll_rows(gain.reshape(clips, -1), mine)
    gain = gain[:1] + sum(send(gain[by : by + 1], "clip", clips, by) for by in range(1, clips))
    return key_grad, value_grad[:ROWS], gain[0]


def body(queries, grad_out, kept_pos, kept_count, caption_len, cap_keys, cap_values, query_gain):
    z, yh, x = (lax.axis_index(name) for name in SEQ)
    feat = queries.shape[-1]
    cap = cap_keys.shape[1] * NZ * NY * NX
    count = lax.dynamic_index_in_dim(kept_count[0], (z * NY + yh) * NX + x, keepdims=False)
    scalars = jnp.stack([count, x])
    slot = jnp.arange(cap, dtype=jnp.int32)[:, None]
    at_z, at_x, at_y = (z + slot // ZROWS) % NZ, (x + slot // UNIT) % NX, slot // ROWS % NY
    caption = ((at_z * NY + at_y) * NX + at_x) * ROWS + slot % ROWS
    bias = jnp.where(caption < caption_len[0], 0.0, -jnp.inf).astype(F32)
    key_parts, values = gather(cap_keys[0], cap_values[0])
    run = lambda head, heads, v, before: grads(
        head, heads, scalars, queries[0], grad_out[0], query_gain[None], kept_pos, bias, v, key_parts,
        before,
    )
    values = spread(values, ("x", "yh"), NXY)
    *kept, far1, dv1 = run(0, CHUNKS[0], values, None)
    *kept, far1, dv1, values = lax.optimization_barrier((*kept, far1, dv1, values))
    *kept, far2, dv2 = run(CHUNKS[0], CHUNKS[1], values, kept)
    dv1, far1 = exchange(dv1, ("x", "yh")), send(far1, "z", NZ, FAR)
    *kept, far2, dv2, dv1, far1 = lax.optimization_barrier((*kept, far2, dv2, dv1, far1))
    query_grad, *terms = kept
    key_grad, value_grad, gain_grad = scatter(*terms, (far1, far2), dv1, dv2)
    return query_grad[None], key_grad.astype(BF16)[None], value_grad.astype(BF16)[None], gain_grad


def solution(mesh):
    parts = Mesh(mesh.devices.reshape(-1, NZ, NY, NX), ("clip",) + SEQ)
    return jax.shard_map(
        body,
        mesh=parts,
        in_specs=(
            P("clip", SEQ, None),
            P("clip", SEQ, None),
            P("clip", SEQ),
            P("clip", None),
            P("clip"),
            P("clip", SEQ, None),
            P("clip", SEQ, None),
            P(),
        ),
        out_specs=(P("clip", SEQ, None), P("clip", SEQ, None), P("clip", SEQ, None), P("clip")),
        check_vma=False,
    )
```
